32 devices in a mesh: narrow: 2 (over x), wide: 16 (over z, y, core).
Axes of the slice: x: 2, y: 2, z: 4, core: 2. Of those that a mesh axis runs over, the one named last changes fastest.
Arguments:
- snapshots: float32 [512, 128, 1024], P('narrow', 'wide'), as said below
- start_basis: float32 [512, 64], replicated, may hold values from -6 to 6
Outputs:
- core_part: float32 [64, 128, 1024], P('narrow', 'wide')
The draws below stay inside these ranges and needn't reach their ends.
Inputs may be any that keep to these rules, and one draw needn't show every extreme that they name: `snapshots`: real values; the x fibres have a dominant subspace of dimension 64.
All inputs are finite; a program needn't handle non-finite values.
Results may differ from the reference program's by a relative error of at most 0.0003.
Values sent between devices are 32-bit elements; how exact they have to be, the bound alone decides.
A program may use at most 64 MiB of HBM per device.

```python
import math
import jax
import jax.numpy as jnp
from jax import lax

NX = 512
RANK = 64
ITERS = 3
NY = 128
LS = 1024


def draw_snapshots(key, part):
    key = jax.random.fold_in(key, 11)
    keys = jax.random.split(key, 5)
    mix_rows = jax.random.normal(keys[0], (NX, 2 * RANK), jnp.float32) / math.sqrt(NX)
    codes = jax.random.normal(keys[1], (2 * RANK, NY * LS), jnp.float32)
    strong = jnp.exp(jax.random.uniform(keys[2], (RANK,), jnp.float32, math.log(2.0), math.log(8.0)))
    weak = jax.random.uniform(keys[3], (RANK,), jnp.float32, 0.6, 1.4)
    noise_part = 0.3 * jax.random.normal(keys[4], (NX, NY * LS), jnp.float32)
    levels_all = jnp.concatenate([strong, weak])
    field = jnp.dot(mix_rows * levels_all[None, :], codes, precision=lax.Precision.HIGHEST) + noise_part
    return field.reshape(NX, NY, LS)


def centred(own_key, extent, scale, bound, held_as=jnp.bfloat16):
    return jnp.clip(scale * jax.random.normal(own_key, extent, jnp.float32), -bound, bound).astype(held_as)


def setup_inputs(seed: int = 0) -> dict:
    key_of = jax.random.split(jax.random.key(seed), 3)
    snapshots = draw_snapshots(jax.random.fold_in(key_of[2], 71), 0)
    start_basis = centred(key_of[1], (NX, RANK), 1.0, 6.0, jnp.float32)
    return dict(snapshots=snapshots, start_basis=start_basis)


def refine_basis(factor, start_basis):
    column_basis = start_basis
    for sweep in range(ITERS):
        inner = jnp.dot(factor.T, column_basis, precision=lax.Precision.HIGHEST)
        image_cols = jnp.dot(factor, inner, precision=lax.Precision.HIGHEST)
        small_gram = jnp.dot(image_cols.T, image_cols, precision=lax.Precision.HIGHEST)
        chol_small = jnp.linalg.cholesky(small_gram)
        column_basis = lax.linalg.triangular_solve(chol_small, image_cols, left_side=False, lower=True, transpose_a=True)
    return column_basis

def reference(snapshots, start_basis):
    unfolded = snapshots.reshape(NX, -1)
    gram_acc = jnp.dot(unfolded, unfolded.T, precision=lax.Precision.HIGHEST)
    factor = jnp.linalg.cholesky(gram_acc)
    column_basis = refine_basis(factor, start_basis)
    return jnp.einsum('xr,xyc->ryc', column_basis, snapshots, precision=lax.Precision.HIGHEST)
```

```python
import jax
import jax.numpy as jnp
from jax import lax
from jax.experimental import pallas as pl
from jax.experimental.pallas import tpu as pltpu
from jax.sharding import PartitionSpec as P

ITERS = 3
RANK = 64
MESH = pl.DeviceIdType.MESH
HIGH = lax.Precision.HIGHEST
F32 = jnp.float32
BF16 = jnp.bfloat16

WIDE = 16
HALF = 256
YS = 8
LS = 1024
LH = LS // 2
COLS = YS * LH
CHUNKS = 4
CX = HALF // CHUNKS
UNITS = 2 * CHUNKS


def dot_nt(a, b):
    return lax.dot_general(a, b, (((1,), (1,)), ((), ())), preferred_element_type=F32)


def dot_nn(a, b):
    return jnp.dot(a, b, preferred_element_type=F32)


def split(value):
    hi = value.astype(BF16)
    return hi, (value - hi.astype(F32)).astype(BF16)


def inverse_chol(gram):
    n = gram.shape[0]
    rows = lax.broadcasted_iota(jnp.int32, (n, 2 * n), 0)
    lanes = lax.broadcasted_iota(jnp.int32, (n, 2 * n), 1)
    eye = (lanes == rows + n).astype(F32)
    table = jnp.concatenate([gram, jnp.zeros((n, n), F32)], axis=1) + eye
    for k in range(n - 1):
        row = table[k : k + 1, :]
        column = jnp.broadcast_to(table[:, k : k + 1], (n, 2 * n))
        scaled = row / row[:, k : k + 1]
        table = table - jnp.where(rows > k, column, 0.0) * scaled
    pivots = jnp.sum(jnp.where(lanes == rows, table, 0.0), axis=1, keepdims=True)
    return (table * lax.rsqrt(pivots))[:, n:]


def kernel(s_hbm, start_ref, out_ref, s32, rbuf, shi, slo, rhi, rlo, stage, landed, gathered, acc,
           gram_ref, basis_ref, core_send, core_own, core_land, load_sem, x_send, x_recv, rs_send,
           rs_recv, pair_send, pair_recv, ag_send, ag_recv, core_ssem, core_rsem, own_sem, land_sem):
    n = lax.axis_index("narrow")
    w = lax.axis_index("wide")
    other = 1 - n
    partner = (other, w)

    def plane(d):
        return (n, lax.rem(w + d, WIDE))

    def loads(q):
        return pltpu.make_async_copy(s_hbm.at[:, pl.ds(q * 128, 128)], s32.at[q], load_sem.at[q])

    def send_chunk(k):
        part = pl.ds(k * CX * YS, CX * YS)
        for q in range(LH // 128):
            pltpu.make_async_remote_copy(
                src_ref=s_hbm.at[part, pl.ds(pl.multiple_of(other * LH + q * 128, 128), 128)],
                dst_ref=rbuf.at[q, part], send_sem=x_send.at[k], recv_sem=x_recv.at[k],
                device_id=partner, device_id_type=MESH).start()

    barrier = pltpu.get_barrier_semaphore()
    pl.semaphore_signal(barrier, inc=1, device_id=partner, device_id_type=MESH)

    def greet(d, carry):
        pl.semaphore_signal(barrier, inc=1, device_id=plane(d), device_id_type=MESH)
        return carry

    lax.fori_loop(1, WIDE, greet, 0)
    for q in range(LS // 128):
        loads(q).start()
    pl.semaphore_wait(barrier, WIDE)
    send_chunk(0)
    send_chunk(1)

    my_rows = pl.ds(pl.multiple_of(w * 8, 8), 8)
    gat_own = pl.ds(pl.multiple_of(n * 128 + w * 8, 8), 8)
    gat_other = pl.ds(pl.multiple_of(other * 128 + w * 8, 8), 8)

    def scatter(u):
        def one(d, carry):
            to = lax.rem(w + d, WIDE)
            pltpu.make_async_remote_copy(
                src_ref=stage.at[u, pl.ds(pl.multiple_of(to * 8, 8), 8)],
                dst_ref=landed.at[u, pl.ds(pl.multiple_of((WIDE - 1 - d) * 8, 8), 8)],
                send_sem=rs_send.at[u], recv_sem=rs_recv.at[u],
                device_id=(n, to), device_id_type=MESH).start()
            return carry

        lax.fori_loop(1, WIDE, one, 0)

    def pair_copy(u):
        return pltpu.make_async_remote_copy(
            src_ref=gathered.at[u, gat_own], dst_ref=gathered.at[u, gat_own],
            send_sem=pair_send.at[u], recv_sem=pair_recv.at[u],
            device_id=partner, device_id_type=MESH)

    def spread(u, part):
        def one(d, carry):
            pltpu.make_async_remote_copy(
                src_ref=gathered.at[u, part], dst_ref=gathered.at[u, part],
                send_sem=ag_send.at[u], recv_sem=ag_recv.at[u],
                device_id=plane(d), device_id_type=MESH).start()
            return carry

        lax.fori_loop(1, WIDE, one, 0)

    def bytes_of(ref, sem):
        return pltpu.make_async_copy(ref, ref, sem)

    fifteen = pl.ds(0, (WIDE - 1) * 8)
    thirty = pl.ds(0, 2 * (WIDE - 1) * 8)

    def reduce_own(u):
        bytes_of(landed.at[u, fifteen], rs_recv.at[u]).wait()
        total = stage[u, my_rows, :]
        for d in range(WIDE - 1):
            total = total + landed[u, pl.ds(d * 8, 8), :]
        gathered[u, gat_own, :] = total
        pair_copy(u).start()
        spread(u, gat_own)

    def forward(u):
        pair_copy(u).wait_recv()
        spread(u, gat_other)

    def finish(u):
        bytes_of(gathered.at[u, thirty], ag_recv.at[u]).wait()

    for q in range(LS // 128):
        loads(q).wait()

    def convert(y, carry):
        for q in range(LS // 128):
            hi, lo = split(s32[q, pl.ds(y, HALF, stride=YS), :])
            h, r = divmod(q * 128, LH)
            at = pl.ds(pl.multiple_of(h * COLS + y * LH + r, 128), 128)
            shi[:, at] = hi
            slo[:, at] = lo
        return carry

    lax.fori_loop(0, YS, convert, 0)

    acc[...] = jnp.zeros_like(acc)

    def diagonal(b, carry):
        at = pl.ds(pl.multiple_of(b * 1024, 1024), 1024)
        hi, lo = shi[:, at], slo[:, at]
        acc[...] += dot_nt(hi, hi) + (dot_nt(hi, lo) + dot_nt(lo, hi))
        return carry

    lax.fori_loop(0, 2 * COLS // 1024, diagonal, 0)
    for u in range(CHUNKS):
        for h in range(2):
            stage[u, pl.ds(h * CX, CX), :] = acc[pl.ds(u * CX, CX), pl.ds(h * 128, 128)]
        scatter(u)
    basis_ref[...] = start_ref[...].T
    for u in range(CHUNKS):
        reduce_own(u)
    for u in range(CHUNKS):
        forward(u)

    for k in range(CHUNKS):
        arriving = rbuf.at[:, pl.ds(k * CX * YS, CX * YS)]
        bytes_of(arriving, x_send.at[k]).wait()
        if k + 2 < CHUNKS:
            send_chunk(k + 2)
        bytes_of(arriving, x_recv.at[k]).wait()
        rows = pl.ds(k * CX, CX)
        acc[rows, :] = jnp.zeros((CX, HALF), F32)

        def arrived(y, carry):
            at = pl.ds(pl.multiple_of(y * LH, LH), LH)
            cells = pl.ds(k * CX * YS + y, CX, stride=YS)
            hi, lo = split(jnp.concatenate([rbuf[q, cells, :] for q in range(LH // 128)], axis=1))
            rhi[rows, at] = hi
            rlo[rows, at] = lo
            mine = pl.ds(pl.multiple_of(n * COLS + y * LH, LH), LH)
            ohi, olo = shi[:, mine], slo[:, mine]
            acc[rows, :] += dot_nt(hi, ohi) + (dot_nt(lo, ohi) + dot_nt(hi, olo))
            return carry

        lax.fori_loop(0, YS, arrived, 0)
        u = CHUNKS + k
        for h in range(2):
            stage[u, pl.ds(h * CX, CX), :] = acc[rows, pl.ds(h * 128, 128)]
        scatter(u)
        if k >= 1:
            reduce_own(u - 1)
            forward(u - 1)
    reduce_own(UNITS - 1)
    forward(UNITS - 1)
    for u in range(CHUNKS):
        finish(u)
        for p in range(2):
            for h in range(2):
                gram_ref[pl.ds(p * HALF + u * CX, CX), pl.ds(p * HALF + h * 128, 128)] = (
                    gathered[u, pl.ds(p * 128 + h * CX, CX), :])
    for u in range(CHUNKS, UNITS):
        finish(u)
        for p in range(2):
            for h in range(2):
                gram_ref[pl.ds((1 - p) * HALF + (u - CHUNKS) * CX, CX), pl.ds(p * HALF + h * 128, 128)] = (
                    gathered[u, pl.ds(p * 128 + h * CX, CX), :])
    lower = gram_ref[pl.ds(HALF, HALF), pl.ds(0, HALF)] + gram_ref[pl.ds(0, HALF), pl.ds(HALF, HALF)].T
    gram_ref[pl.ds(HALF, HALF), pl.ds(0, HALF)] = lower
    gram_ref[pl.ds(0, HALF), pl.ds(HALF, HALF)] = lower.T

    def sweep(i, carry):
        image = jnp.dot(basis_ref[...], gram_ref[...], precision=HIGH, preferred_element_type=F32)
        small = lax.dot_general(image, image, (((1,), (1,)), ((), ())), precision=HIGH,
                                preferred_element_type=F32)
        basis_ref[...] = jnp.dot(inverse_chol(small), image, precision=HIGH, preferred_element_type=F32)
        return carry

    lax.fori_loop(0, ITERS, sweep, 0)

    own_hi, own_lo = split(basis_ref[:, pl.ds(pl.multiple_of(n * HALF, HALF), HALF)])
    oth_hi, oth_lo = split(basis_ref[:, pl.ds(pl.multiple_of(other * HALF, HALF), HALF)])
    own_both = jnp.concatenate([own_hi, own_lo], axis=0)
    oth_both = jnp.concatenate([oth_hi, oth_lo], axis=0)
    BL = LH // 2

    def core_copy(b):
        part = pl.ds(b * (BL // 128), BL // 128)
        return pltpu.make_async_remote_copy(
            src_ref=core_send.at[part], dst_ref=core_land.at[part],
            send_sem=core_ssem.at[b], recv_sem=core_rsem.at[b],
            device_id=partner, device_id_type=MESH)

    for b in range(2):
        for y in range(YS):
            mine = pl.ds(pl.multiple_of(n * COLS + y * LH + b * BL, BL), BL)
            theirs = pl.ds(y * LH + b * BL, BL)
            both = dot_nn(own_both, shi[:, mine]) + dot_nn(oth_both, rhi[:, theirs])
            low = dot_nn(own_hi, slo[:, mine]) + dot_nn(oth_hi, rlo[:, theirs])
            res = both[:RANK] + (both[RANK:] + low)
            first, second = res[: RANK // 2], res[RANK // 2 :]
            at = pl.ds(y, RANK // 2, stride=YS)
            for q in range(BL // 128):
                lane = slice(q * 128, (q + 1) * 128)
                to = b * (BL // 128) + q
                core_own[to, at, :] = jnp.where(n == 0, first[:, lane], second[:, lane])
                core_send[to, at, :] = jnp.where(n == 0, second[:, lane], first[:, lane])
        core_copy(b).start()

    def outs(source, half, sem):
        return [pltpu.make_async_copy(
            source.at[q], out_ref.at[:, pl.ds(pl.multiple_of(half * LH + q * 128, 128), 128)], sem.at[q])
            for q in range(LH // 128)]

    own_out = outs(core_own, n, own_sem)
    for copy in own_out:
        copy.start()
    for u in range(UNITS):
        bytes_of(stage.at[u, fifteen], rs_send.at[u]).wait()
        pair_copy(u).wait_send()
        bytes_of(gathered.at[u, thirty], ag_send.at[u]).wait()
    for b in range(2):
        core_copy(b).wait_recv()
    land_out = outs(core_land, other, land_sem)
    for copy in land_out:
        copy.start()
    for b in range(2):
        core_copy(b).wait_send()
    for copy in own_out + land_out:
        copy.wait()


def in_one_kernel(snapshots, start_basis):
    rows = RANK // 2 * YS
    dma = pltpu.SemaphoreType.DMA
    out = pl.pallas_call(
        kernel,
        out_shape=jax.ShapeDtypeStruct((rows, LS), F32),
        in_specs=[pl.BlockSpec(memory_space=pl.ANY), pl.BlockSpec(memory_space=pltpu.VMEM)],
        out_specs=pl.BlockSpec(memory_space=pl.ANY),
        scratch_shapes=[
            pltpu.VMEM((LS // 128, HALF * YS, 128), F32),
            pltpu.VMEM((LH // 128, HALF * YS, 128), F32),
            pltpu.VMEM((HALF, 2 * COLS), BF16),
            pltpu.VMEM((HALF, 2 * COLS), BF16),
            pltpu.VMEM((HALF, COLS), BF16),
            pltpu.VMEM((HALF, COLS), BF16),
            pltpu.VMEM((UNITS, 128, 128), F32),
            pltpu.VMEM((UNITS, 128, 128), F32),
            pltpu.VMEM((UNITS, 256, 128), F32),
            pltpu.VMEM((HALF, HALF), F32),
            pltpu.VMEM((2 * HALF, 2 * HALF), F32),
            pltpu.VMEM((RANK, 2 * HALF), F32),
            pltpu.VMEM((LH // 128, rows, 128), F32),
            pltpu.VMEM((LH // 128, rows, 128), F32),
            pltpu.VMEM((LH // 128, rows, 128), F32),
            dma((LS // 128,)), dma((CHUNKS,)), dma((CHUNKS,)),
            dma((UNITS,)), dma((UNITS,)), dma((UNITS,)), dma((UNITS,)), dma((UNITS,)), dma((UNITS,)),
            dma((2,)), dma((2,)), dma((LH // 128,)), dma((LH // 128,)),
        ],
        compiler_params=pltpu.CompilerParams(
            collective_id=0, has_side_effects=True, vmem_limit_bytes=48 * 1024 * 1024),
    )(snapshots.reshape(HALF * YS, LS), start_basis)
    return out.reshape(RANK // 2, YS, LS)


def with_collectives(snapshots, start_basis):
    whole_x = lax.all_to_all(snapshots, "narrow", split_axis=1, concat_axis=0, tiled=True)
    unfolded = whole_x.reshape(whole_x.shape[0], -1)
    gram = lax.psum(jnp.dot(unfolded, unfolded.T, precision=HIGH), ("narrow", "wide"))
    column_basis = start_basis
    for sweep in range(ITERS):
        image_cols = jnp.dot(gram, column_basis, precision=HIGH)
        small_gram = jnp.dot(image_cols.T, image_cols, precision=HIGH)
        chol_small = jnp.linalg.cholesky(small_gram)
        column_basis = lax.linalg.triangular_solve(
            chol_small, image_cols, left_side=False, lower=True, transpose_a=True)
    partial_core = jnp.einsum("xr,xyc->ryc", column_basis, whole_x, precision=HIGH)
    return lax.all_to_all(partial_core, "narrow", split_axis=0, concat_axis=1, tiled=True)


def solution(mesh):
    whole = mesh.shape["narrow"] == 2 and mesh.shape["wide"] == WIDE
    placed = (P("narrow", "wide", None), P())
    return jax.shard_map(
        in_one_kernel if whole else with_collectives,
        mesh=mesh, in_specs=placed, out_specs=P("narrow", "wide", None), check_vma=False)
```

```python
import jax
import jax.numpy as jnp
from jax import lax
from jax.experimental import pallas as pl
from jax.experimental.pallas import tpu as pltpu
from jax.sharding import PartitionSpec as P

ITERS = 3
RANK = 64
BLOCK = 8
MESH = pl.DeviceIdType.MESH
HIGH = lax.Precision.HIGHEST
F32 = jnp.float32
BF16 = jnp.bfloat16

WIDE = 16
HALF = 256
YS = 8
LS = 1024
LH = LS // 2
COLS = YS * LH
CHUNKS = 4
CX = HALF // CHUNKS
UNITS = 2 * CHUNKS


def dot_nt(a, b):
    return lax.dot_general(a, b, (((1,), (1,)), ((), ())), preferred_element_type=F32)


def dot_nn(a, b):
    return jnp.dot(a, b, preferred_element_type=F32)


def split(value):
    hi = value.astype(BF16)
    return hi, (value - hi.astype(F32)).astype(BF16)


def inverse_chol(gram):
    n = gram.shape[0]
    rows = lax.broadcasted_iota(jnp.int32, (n, 2 * n), 0)
    lanes = lax.broadcasted_iota(jnp.int32, (n, 2 * n), 1)
    eye = (lanes == rows + n).astype(F32)
    table = jnp.concatenate([gram, jnp.zeros((n, n), F32)], axis=1) + eye
    for k in range(0, n, BLOCK):
        row = [table[k + i : k + i + 1, :] for i in range(BLOCK)]
        column = [jnp.broadcast_to(table[:, k + i : k + i + 1], (n, 2 * n)) for i in range(BLOCK)]
        inverse = []
        for i in range(BLOCK):
            inverse.append(1.0 / column[i][k + i : k + i + 1, :])
            for j in range(i + 1, BLOCK):
                ratio = column[i][k + j : k + j + 1, :] * inverse[i]
                row[j] = row[j] - ratio * row[i]
                column[j] = column[j] - ratio * column[i]
        for i in range(BLOCK):
            table = table - jnp.where(rows > k + i, column[i], 0.0) * (row[i] * inverse[i])
    pivots = jnp.sum(jnp.where(lanes == rows, table, 0.0), axis=1, keepdims=True)
    return (table * lax.rsqrt(pivots))[:, n:]


def kernel(s_hbm, start_ref, out_ref, s32, rbuf, shi, slo, rhi, rlo, stage, landed, gathered, acc,
           gram_ref, basis_ref, core_send, core_own, core_land, load_sem, x_send, x_recv, rs_send,
           rs_recv, pair_send, pair_recv, ag_send, ag_recv, core_ssem, core_rsem, own_sem, land_sem):
    n = lax.axis_index("narrow")
    w = lax.axis_index("wide")
    other = 1 - n
    partner = (other, w)

    def plane(d):
        return (n, lax.rem(w + d, WIDE))

    def loads(q):
        return pltpu.make_async_copy(s_hbm.at[:, pl.ds(q * 128, 128)], s32.at[q], load_sem.at[q])

    def send_chunk(k):
        part = pl.ds(k * CX * YS, CX * YS)
        for q in range(LH // 128):
            pltpu.make_async_remote_copy(
                src_ref=s_hbm.at[part, pl.ds(pl.multiple_of(other * LH + q * 128, 128), 128)],
                dst_ref=rbuf.at[q, part], send_sem=x_send.at[k], recv_sem=x_recv.at[k],
                device_id=partner, device_id_type=MESH).start()

    barrier = pltpu.get_barrier_semaphore()
    pl.semaphore_signal(barrier, inc=1, device_id=partner, device_id_type=MESH)

    def greet(d, carry):
        pl.semaphore_signal(barrier, inc=1, device_id=plane(d), device_id_type=MESH)
        return carry

    lax.fori_loop(1, WIDE, greet, 0)
    for q in range(LS // 128):
        loads(q).start()
    pl.semaphore_wait(barrier, WIDE)
    send_chunk(0)

    my_rows = pl.ds(pl.multiple_of(w * 8, 8), 8)
    gat_own = pl.ds(pl.multiple_of(n * 128 + w * 8, 8), 8)
    gat_other = pl.ds(pl.multiple_of(other * 128 + w * 8, 8), 8)

    def scatter(u):
        def one(d, carry):
            to = lax.rem(w + d, WIDE)
            pltpu.make_async_remote_copy(
                src_ref=stage.at[u, pl.ds(pl.multiple_of(to * 8, 8), 8)],
                dst_ref=landed.at[u, pl.ds(pl.multiple_of((WIDE - 1 - d) * 8, 8), 8)],
                send_sem=rs_send.at[u], recv_sem=rs_recv.at[u],
                device_id=(n, to), device_id_type=MESH).start()
            return carry

        lax.fori_loop(1, WIDE, one, 0)

    def pair_copy(u):
        return pltpu.make_async_remote_copy(
            src_ref=gathered.at[u, gat_own], dst_ref=gathered.at[u, gat_own],
            send_sem=pair_send.at[u], recv_sem=pair_recv.at[u],
            device_id=partner, device_id_type=MESH)

    def spread(u, part):
        def one(d, carry):
            pltpu.make_async_remote_copy(
                src_ref=gathered.at[u, part], dst_ref=gathered.at[u, part],
                send_sem=ag_send.at[u], recv_sem=ag_recv.at[u],
                device_id=plane(d), device_id_type=MESH).start()
            return carry

        lax.fori_loop(1, WIDE, one, 0)

    def bytes_of(ref, sem):
        return pltpu.make_async_copy(ref, ref, sem)

    fifteen = pl.ds(0, (WIDE - 1) * 8)
    thirty = pl.ds(0, 2 * (WIDE - 1) * 8)

    def reduce_own(u):
        bytes_of(landed.at[u, fifteen], rs_recv.at[u]).wait()
        total = stage[u, my_rows, :]
        for d in range(WIDE - 1):
            total = total + landed[u, pl.ds(d * 8, 8), :]
        gathered[u, gat_own, :] = total
        pair_copy(u).start()
        spread(u, gat_own)

    def forward(u):
        pair_copy(u).wait_recv()
        spread(u, gat_other)

    def finish(u):
        bytes_of(gathered.at[u, thirty], ag_recv.at[u]).wait()

    for q in range(LS // 128):
        loads(q).wait()

    def convert(y, carry):
        for q in range(LS // 128):
            hi, lo = split(s32[q, pl.ds(y, HALF, stride=YS), :])
            h, r = divmod(q * 128, LH)
            at = pl.ds(pl.multiple_of(h * COLS + y * LH + r, 128), 128)
            shi[:, at] = hi
            slo[:, at] = lo
        return carry

    lax.fori_loop(0, YS, convert, 0)

    acc[...] = jnp.zeros_like(acc)

    def diagonal(b, carry):
        at = pl.ds(pl.multiple_of(b * 1024, 1024), 1024)
        hi, lo = shi[:, at], slo[:, at]
        acc[...] += dot_nt(hi, hi) + (dot_nt(hi, lo) + dot_nt(lo, hi))
        return carry

    lax.fori_loop(0, 2 * COLS // 1024, diagonal, 0)
    for u in range(CHUNKS):
        for h in range(2):
            stage[u, pl.ds(h * CX, CX), :] = acc[pl.ds(u * CX, CX), pl.ds(h * 128, 128)]
        scatter(u)
    send_chunk(1)
    basis_ref[...] = start_ref[...].T
    for u in range(CHUNKS):
        reduce_own(u)

    for k in range(CHUNKS):
        arriving = rbuf.at[:, pl.ds(k * CX * YS, CX * YS)]
        bytes_of(arriving, x_recv.at[k]).wait()
        if k == 1:
            for u in range(CHUNKS):
                forward(u)
        rows = pl.ds(k * CX, CX)
        acc[rows, :] = jnp.zeros((CX, HALF), F32)

        def arrived(y, carry):
            at = pl.ds(pl.multiple_of(y * LH, LH), LH)
            cells = pl.ds(k * CX * YS + y, CX, stride=YS)
            hi, lo = split(jnp.concatenate([rbuf[q, cells, :] for q in range(LH // 128)], axis=1))
            rhi[rows, at] = hi
            rlo[rows, at] = lo
            mine = pl.ds(pl.multiple_of(n * COLS + y * LH, LH), LH)
            ohi, olo = shi[:, mine], slo[:, mine]
            acc[rows, :] += dot_nt(hi, ohi) + (dot_nt(lo, ohi) + dot_nt(hi, olo))
            return carry

        lax.fori_loop(0, YS, arrived, 0)
        u = CHUNKS + k
        for h in range(2):
            stage[u, pl.ds(h * CX, CX), :] = acc[rows, pl.ds(h * 128, 128)]
        scatter(u)
        if k == CHUNKS - 1:
            forward(u - 1)
        reduce_own(u)
        if k + 2 < CHUNKS:
            send_chunk(k + 2)
        if 1 <= k < CHUNKS - 1:
            forward(u - 1)
    forward(UNITS - 1)
    for u in range(CHUNKS):
        finish(u)
        for p in range(2):
            for h in range(2):
                gram_ref[pl.ds(p * HALF + u * CX, CX), pl.ds(p * HALF + h * 128, 128)] = (
                    gathered[u, pl.ds(p * 128 + h * CX, CX), :])
    for u in range(CHUNKS, UNITS):
        finish(u)
        for p in range(2):
            for h in range(2):
                gram_ref[pl.ds((1 - p) * HALF + (u - CHUNKS) * CX, CX), pl.ds(p * HALF + h * 128, 128)] = (
                    gathered[u, pl.ds(p * 128 + h * CX, CX), :])
    lower = gram_ref[pl.ds(HALF, HALF), pl.ds(0, HALF)] + gram_ref[pl.ds(0, HALF), pl.ds(HALF, HALF)].T
    gram_ref[pl.ds(HALF, HALF), pl.ds(0, HALF)] = lower
    gram_ref[pl.ds(0, HALF), pl.ds(HALF, HALF)] = lower.T

    def sweep(i, carry):
        image = jnp.dot(basis_ref[...], gram_ref[...], precision=HIGH, preferred_element_type=F32)
        small = lax.dot_general(image, image, (((1,), (1,)), ((), ())), precision=HIGH,
                                preferred_element_type=F32)
        basis_ref[...] = jnp.dot(inverse_chol(small), image, precision=HIGH, preferred_element_type=F32)
        return carry

    lax.fori_loop(0, ITERS, sweep, 0)

    own_hi, own_lo = split(basis_ref[:, pl.ds(pl.multiple_of(n * HALF, HALF), HALF)])
    oth_hi, oth_lo = split(basis_ref[:, pl.ds(pl.multiple_of(other * HALF, HALF), HALF)])
    own_both = jnp.concatenate([own_hi, own_lo], axis=0)
    oth_both = jnp.concatenate([oth_hi, oth_lo], axis=0)
    BL = LH // 2

    def core_copy(b):
        part = pl.ds(b * (BL // 128), BL // 128)
        return pltpu.make_async_remote_copy(
            src_ref=core_send.at[part], dst_ref=core_land.at[part],
            send_sem=core_ssem.at[b], recv_sem=core_rsem.at[b],
            device_id=partner, device_id_type=MESH)

    for b in range(2):
        for y in range(YS):
            mine = pl.ds(pl.multiple_of(n * COLS + y * LH + b * BL, BL), BL)
            theirs = pl.ds(y * LH + b * BL, BL)
            both = dot_nn(own_both, shi[:, mine]) + dot_nn(oth_both, rhi[:, theirs])
            low = dot_nn(own_hi, slo[:, mine]) + dot_nn(oth_hi, rlo[:, theirs])
            res = both[:RANK] + (both[RANK:] + low)
            first, second = res[: RANK // 2], res[RANK // 2 :]
            at = pl.ds(y, RANK // 2, stride=YS)
            for q in range(BL // 128):
                lane = slice(q * 128, (q + 1) * 128)
                to = b * (BL // 128) + q
                core_own[to, at, :] = jnp.where(n == 0, first[:, lane], second[:, lane])
                core_send[to, at, :] = jnp.where(n == 0, second[:, lane], first[:, lane])
        core_copy(b).start()

    def outs(source, half, sem):
        return [pltpu.make_async_copy(
            source.at[q], out_ref.at[:, pl.ds(pl.multiple_of(half * LH + q * 128, 128), 128)], sem.at[q])
            for q in range(LH // 128)]

    own_out = outs(core_own, n, own_sem)
    for copy in own_out:
        copy.start()
    for k in range(CHUNKS):
        bytes_of(rbuf.at[:, pl.ds(k * CX * YS, CX * YS)], x_send.at[k]).wait()
    for u in range(UNITS):
        bytes_of(stage.at[u, fifteen], rs_send.at[u]).wait()
        pair_copy(u).wait_send()
        bytes_of(gathered.at[u, thirty], ag_send.at[u]).wait()
    for b in range(2):
        core_copy(b).wait_recv()
    land_out = outs(core_land, other, land_sem)
    for copy in land_out:
        copy.start()
    for b in range(2):
        core_copy(b).wait_send()
    for copy in own_out + land_out:
        copy.wait()


def in_one_kernel(snapshots, start_basis):
    rows = RANK // 2 * YS
    dma = pltpu.SemaphoreType.DMA
    out = pl.pallas_call(
        kernel,
        out_shape=jax.ShapeDtypeStruct((rows, LS), F32),
        in_specs=[pl.BlockSpec(memory_space=pl.ANY), pl.BlockSpec(memory_space=pltpu.VMEM)],
        out_specs=pl.BlockSpec(memory_space=pl.ANY),
        scratch_shapes=[
            pltpu.VMEM((LS // 128, HALF * YS, 128), F32),
            pltpu.VMEM((LH // 128, HALF * YS, 128), F32),
            pltpu.VMEM((HALF, 2 * COLS), BF16),
            pltpu.VMEM((HALF, 2 * COLS), BF16),
            pltpu.VMEM((HALF, COLS), BF16),
            pltpu.VMEM((HALF, COLS), BF16),
            pltpu.VMEM((UNITS, 128, 128), F32),
            pltpu.VMEM((UNITS, 128, 128), F32),
            pltpu.VMEM((UNITS, 256, 128), F32),
            pltpu.VMEM((HALF, HALF), F32),
            pltpu.VMEM((2 * HALF, 2 * HALF), F32),
            pltpu.VMEM((RANK, 2 * HALF), F32),
            pltpu.VMEM((LH // 128, rows, 128), F32),
            pltpu.VMEM((LH // 128, rows, 128), F32),
            pltpu.VMEM((LH // 128, rows, 128), F32),
            dma((LS // 128,)), dma((CHUNKS,)), dma((CHUNKS,)),
            dma((UNITS,)), dma((UNITS,)), dma((UNITS,)), dma((UNITS,)), dma((UNITS,)), dma((UNITS,)),
            dma((2,)), dma((2,)), dma((LH // 128,)), dma((LH // 128,)),
        ],
        compiler_params=pltpu.CompilerParams(
            collective_id=0, has_side_effects=True, vmem_limit_bytes=48 * 1024 * 1024),
    )(snapshots.reshape(HALF * YS, LS), start_basis)
    return out.reshape(RANK // 2, YS, LS)


def with_collectives(snapshots, start_basis):
    whole_x = lax.all_to_all(snapshots, "narrow", split_axis=1, concat_axis=0, tiled=True)
    unfolded = whole_x.reshape(whole_x.shape[0], -1)
    gram = lax.psum(jnp.dot(unfolded, unfolded.T, precision=HIGH), ("narrow", "wide"))
    column_basis = start_basis
    for sweep in range(ITERS):
        image_cols = jnp.dot(gram, column_basis, precision=HIGH)
        small_gram = jnp.dot(image_cols.T, image_cols, precision=HIGH)
        chol_small = jnp.linalg.cholesky(small_gram)
        column_basis = lax.linalg.triangular_solve(
            chol_small, image_cols, left_side=False, lower=True, transpose_a=True)
    partial_core = jnp.einsum("xr,xyc->ryc", column_basis, whole_x, precision=HIGH)
    return lax.all_to_all(partial_core, "narrow", split_axis=0, concat_axis=1, tiled=True)


def solution(mesh):
    whole = mesh.shape["narrow"] == 2 and mesh.shape["wide"] == WIDE
    placed = (P("narrow", "wide", None), P())
    return jax.shard_map(
        in_one_kernel if whole else with_collectives,
        mesh=mesh, in_specs=placed, out_specs=P("narrow", "wide", None), check_vma=False)
```

```python
import jax
import jax.numpy as jnp
from jax import lax
from jax.experimental import pallas as pl
from jax.experimental.pallas import tpu as pltpu
from jax.sharding import PartitionSpec as P

ITERS = 3
RANK = 64
BLOCK = 8
MESH = pl.DeviceIdType.MESH
HIGH = lax.Precision.HIGHEST
F32 = jnp.float32
BF16 = jnp.bfloat16

WIDE = 16
HALF = 256
YS = 8
LS = 1024
LH = LS // 2
COLS = YS * LH
CHUNKS = 4
CX = HALF // CHUNKS
UNITS = 2 * CHUNKS


def dot_nt(a, b):
    return lax.dot_general(a, b, (((1,), (1,)), ((), ())), preferred_element_type=F32)


def dot_nn(a, b):
    return jnp.dot(a, b, preferred_element_type=F32)


def split(value):
    hi = value.astype(BF16)
    return hi, (value - hi.astype(F32)).astype(BF16)


def inverse_chol(gram):
    n = gram.shape[0]
    rows = lax.broadcasted_iota(jnp.int32, (n, 2 * n), 0)
    lanes = lax.broadcasted_iota(jnp.int32, (n, 2 * n), 1)
    eye = (lanes == rows + n).astype(F32)
    table = jnp.concatenate([gram, jnp.zeros((n, n), F32)], axis=1) + eye
    for k in range(0, n, BLOCK):
        row = [table[k + i : k + i + 1, :] for i in range(BLOCK)]
        column = [jnp.broadcast_to(table[:, k + i : k + i + 1], (n, 2 * n)) for i in range(BLOCK)]
        inverse = []
        for i in range(BLOCK):
            inverse.append(1.0 / column[i][k + i : k + i + 1, :])
            for j in range(i + 1, BLOCK):
                ratio = column[i][k + j : k + j + 1, :] * inverse[i]
                row[j] = row[j] - ratio * row[i]
                column[j] = column[j] - ratio * column[i]
        for i in range(BLOCK):
            table = table - jnp.where(rows > k + i, column[i], 0.0) * (row[i] * inverse[i])
    pivots = jnp.sum(jnp.where(lanes == rows, table, 0.0), axis=1, keepdims=True)
    return (table * lax.rsqrt(pivots))[:, n:]


def kernel(s_hbm, start_ref, out_ref, s32, rbuf, shi, slo, rhi, rlo, stage, landed, gathered, acc,
           gram_ref, basis_ref, core_send, core_own, core_land, load_sem, x_send, x_recv, rs_send,
           rs_recv, pair_send, pair_recv, ag_send, ag_recv, core_ssem, core_rsem, own_sem, land_sem):
    n = lax.axis_index("narrow")
    w = lax.axis_index("wide")
    other = 1 - n
    partner = (other, w)

    def plane(d):
        return (n, lax.rem(w + d, WIDE))

    def loads(q):
        return pltpu.make_async_copy(s_hbm.at[:, pl.ds(q * 128, 128)], s32.at[q], load_sem.at[q])

    def send_chunk(k):
        part = pl.ds(k * CX * YS, CX * YS)
        for q in range(LH // 128):
            pltpu.make_async_remote_copy(
                src_ref=s_hbm.at[part, pl.ds(pl.multiple_of(other * LH + q * 128, 128), 128)],
                dst_ref=rbuf.at[q, part], send_sem=x_send.at[k], recv_sem=x_recv.at[k, q],
                device_id=partner, device_id_type=MESH).start()

    barrier = pltpu.get_barrier_semaphore()
    pl.semaphore_signal(barrier, inc=1, device_id=partner, device_id_type=MESH)

    def greet(d, carry):
        pl.semaphore_signal(barrier, inc=1, device_id=plane(d), device_id_type=MESH)
        return carry

    lax.fori_loop(1, WIDE, greet, 0)
    for q in range(LS // 128):
        loads(q).start()
    pl.semaphore_wait(barrier, WIDE)
    send_chunk(0)

    my_rows = pl.ds(pl.multiple_of(w * 8, 8), 8)
    gat_own = pl.ds(pl.multiple_of(n * 128 + w * 8, 8), 8)
    gat_other = pl.ds(pl.multiple_of(other * 128 + w * 8, 8), 8)

    def scatter(u):
        def one(d, carry):
            to = lax.rem(w + d, WIDE)
            pltpu.make_async_remote_copy(
                src_ref=stage.at[u, pl.ds(pl.multiple_of(to * 8, 8), 8)],
                dst_ref=landed.at[u, pl.ds(pl.multiple_of((WIDE - 1 - d) * 8, 8), 8)],
                send_sem=rs_send.at[u], recv_sem=rs_recv.at[u],
                device_id=(n, to), device_id_type=MESH).start()
            return carry

        lax.fori_loop(1, WIDE, one, 0)

    def pair_copy(u):
        return pltpu.make_async_remote_copy(
            src_ref=gathered.at[u, gat_own], dst_ref=gathered.at[u, gat_own],
            send_sem=pair_send.at[u], recv_sem=pair_recv.at[u],
            device_id=partner, device_id_type=MESH)

    def spread(u, part):
        def one(d, carry):
            pltpu.make_async_remote_copy(
                src_ref=gathered.at[u, part], dst_ref=gathered.at[u, part],
                send_sem=ag_send.at[u], recv_sem=ag_recv.at[u],
                device_id=plane(d), device_id_type=MESH).start()
            return carry

        lax.fori_loop(1, WIDE, one, 0)

    def bytes_of(ref, sem):
        return pltpu.make_async_copy(ref, ref, sem)

    fifteen = pl.ds(0, (WIDE - 1) * 8)
    thirty = pl.ds(0, 2 * (WIDE - 1) * 8)

    def reduce_own(u):
        bytes_of(landed.at[u, fifteen], rs_recv.at[u]).wait()
        total = stage[u, my_rows, :]
        for d in range(WIDE - 1):
            total = total + landed[u, pl.ds(d * 8, 8), :]
        gathered[u, gat_own, :] = total
        pair_copy(u).start()
        spread(u, gat_own)

    def forward(u):
        pair_copy(u).wait_recv()
        spread(u, gat_other)

    def finish(u):
        bytes_of(gathered.at[u, thirty], ag_recv.at[u]).wait()

    for q in range(LS // 128):
        loads(q).wait()

    def convert(y, carry):
        for q in range(LS // 128):
            hi, lo = split(s32[q, pl.ds(y, HALF, stride=YS), :])
            h, r = divmod(q * 128, LH)
            at = pl.ds(pl.multiple_of(h * COLS + y * LH + r, 128), 128)
            shi[:, at] = hi
            slo[:, at] = lo
        return carry

    lax.fori_loop(0, YS, convert, 0)

    acc[...] = jnp.zeros_like(acc)

    def diagonal(b, carry):
        at = pl.ds(pl.multiple_of(b * 1024, 1024), 1024)
        hi, lo = shi[:, at], slo[:, at]
        acc[...] += dot_nt(hi, hi) + (dot_nt(hi, lo) + dot_nt(lo, hi))
        return carry

    lax.fori_loop(0, 2 * COLS // 1024, diagonal, 0)
    for u in range(CHUNKS):
        for h in range(2):
            stage[u, pl.ds(h * CX, CX), :] = acc[pl.ds(u * CX, CX), pl.ds(h * 128, 128)]
        scatter(u)
    send_chunk(1)
    basis_ref[...] = start_ref[...].T
    for u in range(CHUNKS):
        reduce_own(u)

    for k in range(CHUNKS):
        part = pl.ds(k * CX * YS, CX * YS)
        if k == 1:
            for u in range(CHUNKS):
                forward(u)
        rows = pl.ds(k * CX, CX)
        acc[rows, :] = jnp.zeros((CX, HALF), F32)

        for q in range(LH // 128):
            bytes_of(rbuf.at[q, part], x_recv.at[k, q]).wait()
            his, los, ohis, olos = [], [], [], []
            for y in range(YS):
                hi, lo = split(rbuf[q, pl.ds(k * CX * YS + y, CX, stride=YS), :])
                at = pl.ds(y * LH + q * 128, 128)
                rhi[rows, at] = hi
                rlo[rows, at] = lo
                mine = pl.ds(pl.multiple_of(n * COLS + y * LH + q * 128, 128), 128)
                his.append(hi)
                los.append(lo)
                ohis.append(shi[:, mine])
                olos.append(slo[:, mine])
            hi, lo, ohi, olo = (jnp.concatenate(v, axis=1) for v in (his, los, ohis, olos))
            acc[rows, :] += dot_nt(hi, ohi) + (dot_nt(lo, ohi) + dot_nt(hi, olo))
        u = CHUNKS + k
        for h in range(2):
            stage[u, pl.ds(h * CX, CX), :] = acc[rows, pl.ds(h * 128, 128)]
        scatter(u)
        if k == CHUNKS - 1:
            forward(u - 1)
        reduce_own(u)
        if k + 2 < CHUNKS:
            send_chunk(k + 2)
        if 1 <= k < CHUNKS - 1:
            forward(u - 1)
    forward(UNITS - 1)
    for u in range(CHUNKS):
        finish(u)
        for p in range(2):
            for h in range(2):
                gram_ref[pl.ds(p * HALF + u * CX, CX), pl.ds(p * HALF + h * 128, 128)] = (
                    gathered[u, pl.ds(p * 128 + h * CX, CX), :])
    for u in range(CHUNKS, UNITS):
        finish(u)
        for p in range(2):
            for h in range(2):
                gram_ref[pl.ds((1 - p) * HALF + (u - CHUNKS) * CX, CX), pl.ds(p * HALF + h * 128, 128)] = (
                    gathered[u, pl.ds(p * 128 + h * CX, CX), :])
    lower = gram_ref[pl.ds(HALF, HALF), pl.ds(0, HALF)] + gram_ref[pl.ds(0, HALF), pl.ds(HALF, HALF)].T
    gram_ref[pl.ds(HALF, HALF), pl.ds(0, HALF)] = lower
    gram_ref[pl.ds(0, HALF), pl.ds(HALF, HALF)] = lower.T

    def sweep(i, carry):
        image = jnp.dot(basis_ref[...], gram_ref[...], precision=HIGH, preferred_element_type=F32)
        small = lax.dot_general(image, image, (((1,), (1,)), ((), ())), precision=HIGH,
                                preferred_element_type=F32)
        basis_ref[...] = jnp.dot(inverse_chol(small), image, precision=HIGH, preferred_element_type=F32)
        return carry

    lax.fori_loop(0, ITERS, sweep, 0)

    own_hi, own_lo = split(basis_ref[:, pl.ds(pl.multiple_of(n * HALF, HALF), HALF)])
    oth_hi, oth_lo = split(basis_ref[:, pl.ds(pl.multiple_of(other * HALF, HALF), HALF)])
    own_both = jnp.concatenate([own_hi, own_lo], axis=0)
    oth_both = jnp.concatenate([oth_hi, oth_lo], axis=0)
    BL = LH // 2

    def core_copy(b):
        part = pl.ds(b * (BL // 128), BL // 128)
        return pltpu.make_async_remote_copy(
            src_ref=core_send.at[part], dst_ref=core_land.at[part],
            send_sem=core_ssem.at[b], recv_sem=core_rsem.at[b],
            device_id=partner, device_id_type=MESH)

    for b in range(2):
        for y in range(YS):
            mine = pl.ds(pl.multiple_of(n * COLS + y * LH + b * BL, BL), BL)
            theirs = pl.ds(y * LH + b * BL, BL)
            both = dot_nn(own_both, shi[:, mine]) + dot_nn(oth_both, rhi[:, theirs])
            low = dot_nn(own_hi, slo[:, mine]) + dot_nn(oth_hi, rlo[:, theirs])
            res = both[:RANK] + (both[RANK:] + low)
            first, second = res[: RANK // 2], res[RANK // 2 :]
            at = pl.ds(y, RANK // 2, stride=YS)
            for q in range(BL // 128):
                lane = slice(q * 128, (q + 1) * 128)
                to = b * (BL // 128) + q
                core_own[to, at, :] = jnp.where(n == 0, first[:, lane], second[:, lane])
                core_send[to, at, :] = jnp.where(n == 0, second[:, lane], first[:, lane])
        core_copy(b).start()

    def outs(source, half, sem):
        return [pltpu.make_async_copy(
            source.at[q], out_ref.at[:, pl.ds(pl.multiple_of(half * LH + q * 128, 128), 128)], sem.at[q])
            for q in range(LH // 128)]

    own_out = outs(core_own, n, own_sem)
    for copy in own_out:
        copy.start()
    for k in range(CHUNKS):
        bytes_of(rbuf.at[:, pl.ds(k * CX * YS, CX * YS)], x_send.at[k]).wait()
    for u in range(UNITS):
        bytes_of(stage.at[u, fifteen], rs_send.at[u]).wait()
        pair_copy(u).wait_send()
        bytes_of(gathered.at[u, thirty], ag_send.at[u]).wait()
    land_out = outs(core_land, other, land_sem)
    for b in range(2):
        core_copy(b).wait_recv()
        for copy in land_out[b * (BL // 128) : (b + 1) * (BL // 128)]:
            copy.start()
    for b in range(2):
        core_copy(b).wait_send()
    for copy in own_out + land_out:
        copy.wait()


def in_one_kernel(snapshots, start_basis):
    rows = RANK // 2 * YS
    dma = pltpu.SemaphoreType.DMA
    out = pl.pallas_call(
        kernel,
        out_shape=jax.ShapeDtypeStruct((rows, LS), F32),
        in_specs=[pl.BlockSpec(memory_space=pl.ANY), pl.BlockSpec(memory_space=pltpu.VMEM)],
        out_specs=pl.BlockSpec(memory_space=pl.ANY),
        scratch_shapes=[
            pltpu.VMEM((LS // 128, HALF * YS, 128), F32),
            pltpu.VMEM((LH // 128, HALF * YS, 128), F32),
            pltpu.VMEM((HALF, 2 * COLS), BF16),
            pltpu.VMEM((HALF, 2 * COLS), BF16),
            pltpu.VMEM((HALF, COLS), BF16),
            pltpu.VMEM((HALF, COLS), BF16),
            pltpu.VMEM((UNITS, 128, 128), F32),
            pltpu.VMEM((UNITS, 128, 128), F32),
            pltpu.VMEM((UNITS, 256, 128), F32),
            pltpu.VMEM((HALF, HALF), F32),
            pltpu.VMEM((2 * HALF, 2 * HALF), F32),
            pltpu.VMEM((RANK, 2 * HALF), F32),
            pltpu.VMEM((LH // 128, rows, 128), F32),
            pltpu.VMEM((LH // 128, rows, 128), F32),
            pltpu.VMEM((LH // 128, rows, 128), F32),
            dma((LS // 128,)), dma((CHUNKS,)), dma((CHUNKS, LH // 128)),
            dma((UNITS,)), dma((UNITS,)), dma((UNITS,)), dma((UNITS,)), dma((UNITS,)), dma((UNITS,)),
            dma((2,)), dma((2,)), dma((LH // 128,)), dma((LH // 128,)),
        ],
        compiler_params=pltpu.CompilerParams(
            collective_id=0, has_side_effects=True, vmem_limit_bytes=48 * 1024 * 1024),
    )(snapshots.reshape(HALF * YS, LS), start_basis)
    return out.reshape(RANK // 2, YS, LS)


def with_collectives(snapshots, start_basis):
    whole_x = lax.all_to_all(snapshots, "narrow", split_axis=1, concat_axis=0, tiled=True)
    unfolded = whole_x.reshape(whole_x.shape[0], -1)
    gram = lax.psum(jnp.dot(unfolded, unfolded.T, precision=HIGH), ("narrow", "wide"))
    column_basis = start_basis
    for sweep in range(ITERS):
        image_cols = jnp.dot(gram, column_basis, precision=HIGH)
        small_gram = jnp.dot(image_cols.T, image_cols, precision=HIGH)
        chol_small = jnp.linalg.cholesky(small_gram)
        column_basis = lax.linalg.triangular_solve(
            chol_small, image_cols, left_side=False, lower=True, transpose_a=True)
    partial_core = jnp.einsum("xr,xyc->ryc", column_basis, whole_x, precision=HIGH)
    return lax.all_to_all(partial_core, "narrow", split_axis=0, concat_axis=1, tiled=True)


def solution(mesh):
    whole = mesh.shape["narrow"] == 2 and mesh.shape["wide"] == WIDE
    placed = (P("narrow", "wide", None), P())
    return jax.shard_map(
        in_one_kernel if whole else with_collectives,
        mesh=mesh, in_specs=placed, out_specs=P("narrow", "wide", None), check_vma=False)
```
